256 devices in a mesh: fsdp: 4 (over x_lo, core), dp: 64 (over x_hi, y, z).
Axes of the slice: x: 4 (x_hi: 2, x_lo: 2; x = x_hi * 2 + x_lo), y: 4, z: 8, core: 2. Of those that a mesh axis runs over, the one named last changes fastest.
Arguments:
- inputs: bfloat16 [32768, 2048], P('dp', 'fsdp'), may hold values from -16 to 16
- cotangent: bfloat16 [32768, 7168], P('dp', 'fsdp'), may hold values from -6 to 6
- weight: bfloat16 [2048, 7168], P(None, 'fsdp'), may hold values from -0.125 to 0.125
- master: float32 [2048, 7168], P('dp', 'fsdp'), may hold values from -0.125 to 0.125
- first_moment: float32 [2048, 7168], P('dp', 'fsdp'), may hold values from -6 to 6
- second_moment: float32 [2048, 7168], P('dp', 'fsdp'), may hold values from 0.1 to 0.4
Outputs:
- input_grad: bfloat16 [32768, 2048], P('dp', 'fsdp')
- new_master: float32 [2048, 7168], P('dp', 'fsdp')
- new_first: float32 [2048, 7168], P('dp', 'fsdp')
- new_second: float32 [2048, 7168], P('dp', 'fsdp')
The draws below stay inside these ranges and needn't reach their ends.
All inputs are finite; a program needn't handle non-finite values.
Results may differ from the reference program's by a relative error of at most 0.00055.
Values may be sent and summed in bfloat16 or wider, within the bound.
A program may use at most 128 MiB of HBM per device.

```python
import math
import jax
import jax.numpy as jnp

D = 2048
FF = 7168
TOKENS = 32768


def spiked(array, stream_key, source, target, parts, factor):
    owner, partner = [(jnp.arange(array.shape[dim]) // (array.shape[dim] // parts)).reshape([-1 if axis == dim else 1 for axis in range(array.ndim)]) for dim in (source, target)]
    chosen = jax.random.permutation(stream_key, parts)[partner]
    strong = (owner == chosen) | (owner == (partner + parts // 2) % parts)
    return jnp.where(strong, factor * array, array)


def steps_of(own_key, shape, pieces, smallest, largest):
    loudness, own = 1.0, jax.random.fold_in(own_key, 6)
    for position, shards_of in pieces:
        heights = jnp.exp(jax.random.uniform(jax.random.fold_in(own, position), (shards_of,), jnp.float32, smallest / len(pieces), largest / len(pieces)))
        loudness = loudness * jnp.repeat(heights, shape[position] // shards_of).reshape([-1 if axis == position else 1 for axis in range(len(shape))])
    return loudness


def centred(stream_key, extent, scale, reach, shards=(), held_as=jnp.bfloat16):
    loudness = steps_of(stream_key, extent, shards, -0.22, 0.18) if shards else 1.0
    entries = jax.random.normal(stream_key, extent, jnp.float32) * scale * loudness
    return jnp.minimum(jnp.maximum(entries, -reach), reach).astype(held_as)


def gaussian_with(stream_key, extent, deviation, limit, cuts, heavy, held_as=jnp.bfloat16):
    drawn = deviation * jax.random.normal(stream_key, extent, jnp.float32)
    if cuts:
        drawn = drawn * steps_of(stream_key, extent, cuts, -0.22, 0.18)
    return jnp.clip(spiked(drawn, jax.random.fold_in(stream_key, 3), *heavy), -limit, limit).astype(held_as)


def setup_inputs(seed: int = 0) -> dict:
    keys = jax.random.split(jax.random.key(seed), 7)
    inputs = gaussian_with(keys[0], (TOKENS, D), 1.0, 16.0, ((0, 64), (1, 4)), (0, 1, 64, 4.0))
    cotangent = centred(keys[1], (TOKENS, FF), 1.0, 6.0, ((0, 64), (1, 4)))
    weight = centred(keys[2], (D, FF), D ** -0.5, 0.125, ((1, 4),))
    master = centred(keys[3], (D, FF), D ** -0.5, 0.125, ((0, 64), (1, 4)), jnp.float32)
    first_moment = centred(keys[4], (D, FF), 1.0, 6.0, ((0, 64), (1, 4)), jnp.float32)
    second_moment = jnp.clip(jnp.exp(math.log(0.4) - 1.3862944 * jax.random.uniform(keys[5], (D, FF), jnp.float32) ** steps_of(keys[5], (D, FF), ((0, 64), (1, 4)), -0.2, 0.2)), 0.1, 0.4)
    return dict(inputs=inputs, cotangent=cotangent, weight=weight, master=master, first_moment=first_moment, second_moment=second_moment)


def adamw_update(grad, master, first_moment, second_moment):
    new_first = 0.9 * first_moment + 0.1 * grad
    new_second = 0.95 * second_moment + 0.05 * grad * grad
    corrected = new_first / (1.0 - 0.9 ** 10) / (jnp.sqrt(new_second / (1.0 - 0.95 ** 10)) + 1e-08)
    new_master = master - 0.001 * (corrected + 0.1 * master)
    return (new_master, new_first, new_second)

def reference(inputs, cotangent, weight, master, first_moment, second_moment):
    input_grad = jnp.dot(cotangent, weight.T, preferred_element_type=jnp.float32).astype(jnp.bfloat16)
    grad = jnp.dot(inputs.T, cotangent, preferred_element_type=jnp.float32) * float(TOKENS) ** (-0.5)
    new_master, new_first, new_second = adamw_update(grad, master, first_moment, second_moment)
    return (input_grad, new_master, new_first, new_second)
```

```python
import jax
import jax.numpy as jnp
from jax import lax
from jax.experimental import pallas as pl
from jax.experimental.pallas import tpu as pltpu
from jax.sharding import PartitionSpec as P

MESH = pl.DeviceIdType.MESH
F32, BF16 = jnp.float32, jnp.bfloat16
TOK, FEAT, COLS = 512, 512, 1792
LIFT = 1024.0
STREAMS = (
    (("a", 384), ("a", 256), ("a", 384), ("h", 768)),
    (("a", 512), ("a", 512), ("b", 256), ("b", 512)),
)
ORDER = (
    ("sendx",), ("ig0",), ("mg", 0, 3, 0), ("mg", 0, 2, 1), ("hz0", 0, 3, "o", 1), ("hz0", 0, 3, "m", 0),
    ("mg", 0, 2, 0), ("ay", 0, 2, "o", 1), ("mg", 0, 1, 1), ("mg", 0, 3, 1), ("mg", 0, 1, 0),
    ("ay", 0, 1, "m", 0), ("mg", 0, 0, 0), ("hz1", 0, 3, "m", 0), ("ay", 0, 2, "m", 0),
    ("hz1", 0, 3, "o", 1), ("ay", 0, 1, "o", 1), ("ig1",), ("iadd",), ("hz0", 0, 3, "o", 2),
    ("mg", 0, 0, 1), ("ay", 0, 0, "m", 0), ("hz0", 0, 3, "m", 1), ("ay", 0, 0, "o", 1),
    ("hz1", 0, 3, "o", 2), ("ay", 0, 1, "m", 1), ("hz1", 0, 3, "m", 1), ("ig2",), ("hz0", 0, 3, "o", 3),
    ("ig3",), ("ay", 0, 2, "m", 1), ("fwd",), ("mg", 1, 3, 0), ("mg", 1, 2, 0), ("mg", 1, 0, 0),
    ("hz1", 0, 3, "o", 3), ("hz0", 0, 3, "m", 2), ("mg", 1, 1, 0), ("mg", 1, 3, 1), ("bz", 1, 3, "o", 1),
    ("mg", 1, 1, 1), ("ay", 0, 0, "m", 1), ("mg", 1, 2, 1), ("bz", 1, 3, "m", 0), ("ay", 1, 1, "o", 1),
    ("bz", 1, 2, "m", 0), ("ay", 1, 1, "m", 0), ("mg", 1, 0, 1), ("ay", 1, 0, "m", 0), ("bz", 1, 2, "o", 1),
    ("ay", 0, 2, "f"), ("az", 0, 2, "m", 0), ("ay", 0, 1, "f"), ("xo", 0, 1), ("hz0", 0, 3, "m", 3),
    ("ay", 1, 0, "o", 1), ("hz1", 0, 3, "m", 2), ("bz", 1, 3, "o", 2), ("az", 0, 2, "o", 1),
    ("az", 0, 1, "o", 1), ("az", 0, 1, "m", 0), ("xo", 0, 2), ("bz", 1, 3, "m", 1), ("ay", 0, 0, "f"),
    ("az", 0, 0, "m", 0), ("bz", 1, 2, "m", 1), ("bz", 1, 2, "o", 2), ("az", 0, 2, "m", 1), ("xo", 0, 0),
    ("az", 0, 0, "o", 1), ("hz0", 0, 3, "f"), ("bz", 1, 3, "o", 3), ("az", 0, 2, "o", 2),
    ("az", 0, 1, "o", 2), ("hz1", 0, 3, "m", 3), ("az", 0, 1, "m", 1), ("ay", 1, 1, "m", 1),
    ("bz", 1, 2, "o", 3), ("az", 0, 0, "o", 2), ("bz", 1, 3, "m", 2), ("az", 0, 0, "m", 1),
    ("az", 0, 2, "o", 3), ("ay", 1, 0, "m", 1), ("bz", 1, 2, "m", 2), ("az", 0, 1, "o", 3),
    ("az", 0, 2, "m", 2), ("ifin",), ("az", 0, 0, "o", 3), ("hz1", 0, 3, "f"), ("az", 0, 1, "m", 2),
    ("by", 0, 3, "m", 0), ("ay", 1, 1, "f"), ("az", 1, 1, "o", 1), ("az", 1, 1, "m", 0),
    ("by", 0, 3, "o", 1), ("xo", 1, 1), ("xo", 0, 3), ("bz", 1, 3, "m", 3), ("az", 0, 0, "m", 2),
    ("ay", 1, 0, "f"), ("az", 1, 0, "m", 0), ("bz", 1, 2, "m", 3), ("by", 0, 3, "m", 1),
    ("az", 0, 2, "m", 3), ("az", 1, 1, "o", 2), ("az", 0, 1, "m", 3), ("az", 1, 1, "m", 1),
    ("az", 1, 0, "o", 1), ("xo", 1, 0), ("bz", 1, 3, "f"), ("by", 1, 3, "m", 0), ("az", 0, 0, "m", 3),
    ("xo", 1, 3), ("by", 1, 3, "o", 1), ("az", 1, 0, "m", 1), ("az", 1, 1, "o", 3), ("by", 0, 3, "f"),
    ("az", 1, 0, "o", 2), ("bz", 1, 2, "f"), ("by", 1, 2, "m", 0), ("xo", 1, 2), ("by", 1, 2, "o", 1),
    ("az", 1, 1, "m", 2), ("by", 1, 3, "m", 1), ("az", 0, 2, "f"), ("az", 1, 0, "m", 2), ("az", 0, 1, "f"),
    ("az", 0, 0, "f"), ("az", 1, 0, "o", 3), ("by", 1, 2, "m", 1), ("az", 1, 1, "m", 3),
    ("az", 1, 0, "m", 3), ("by", 1, 3, "f"), ("by", 1, 2, "f"), ("az", 1, 1, "f"), ("az", 1, 0, "f"),
)


def encode(x):
    s = x * x
    return (s * (x * jnp.abs(x))).astype(BF16)


def decode(c):
    c = c.astype(F32)
    t = lax.rsqrt(lax.rsqrt(jnp.abs(c)))
    return jnp.where(c < 0, -t, t)


def adamw_update(grad, master, first_moment, second_moment):
    new_first = 0.9 * first_moment + 0.1 * grad
    new_second = 0.95 * second_moment + 0.05 * grad * grad
    corrected = new_first / (1.0 - 0.9**10) / (jnp.sqrt(new_second / (1.0 - 0.95**10)) + 1e-08)
    new_master = master - 0.001 * (corrected + 0.1 * master)
    return (new_master, new_first, new_second)


STAGES = {"a": ("ay", "az"), "b": ("bz", "by"), "h": ("hz0", "hz1", "by")}
RING = {"ay": (4, 8), "az": (8, 1), "bz": (8, 4), "hz0": (8, 2), "hz1": (8, 2), "by": (4, 1)}
LAST = ("az", "by")


def streams():
    for ph, cut in enumerate(STREAMS):
        first = 0
        for s, (kind, width) in enumerate(cut):
            yield ph, s, kind, first, width
            first += width


def kernel(norm, x_hbm, c_hbm, w_hbm, grad_out, ig_out, *scratch):
    x_in, xt, cot, w, g, pc_s, pc_r, pp_s, pp_r = scratch[:9]
    ld_sem, xt_ss, xt_rs, pc_ss, pc_rs, pp_ss, pp_rs = scratch[9:16]
    rest = list(scratch[16:])
    buffers = {}
    spans = {}
    for ph, s, kind, first, width in streams():
        spans[ph, s] = pl.ds(first, width), width
        for stage in STAGES[kind]:
            buffers[stage, ph, s], rest = rest[:4], rest[4:]

    f, d = lax.axis_index("fsdp"), lax.axis_index("dp")
    x_lo, core = f // 2, f % 2
    x_hi, y, z = d // 32, (d // 8) % 4, d % 8
    turn = 1 - 2 * core
    mine = (x_lo + x_hi) % 2
    other_core = {"dp": d, "fsdp": x_lo * 2 + (1 - core)}
    x_lo_peer = {"dp": d, "fsdp": (1 - x_lo) * 2 + core}
    x_hi_peer = {"dp": (1 - x_hi) * 32 + y * 8 + z, "fsdp": f}

    def y_peer(step, across=0):
        return {"dp": (x_hi + across) % 2 * 32 + ((y + 4 + step) % 4) * 8 + z, "fsdp": f}

    def z_peer(step, across=0):
        return {"dp": (x_hi + across) % 2 * 32 + y * 8 + (z + 8 + step) % 8, "fsdp": f}

    barrier = pltpu.get_barrier_semaphore()
    partners = [other_core, x_lo_peer, x_hi_peer]
    partners += [peer(step, side) for peer in (y_peer, z_peer) for step in (1, -1) for side in (0, 1)]
    for p in partners:
        pl.semaphore_signal(barrier, inc=1, device_id=p, device_id_type=MESH)
    load_x = pltpu.make_async_copy(x_hbm, x_in, ld_sem.at[0])
    load_x.start()
    load_c = pltpu.make_async_copy(c_hbm, cot, ld_sem.at[1])
    load_c.start()
    blocks = ((1 - x_lo) * 2 + (1 - core), (1 - x_lo) * 2 + core, x_lo * 2 + (1 - core), f)
    load_w = []
    for i, b in enumerate(blocks):
        copy = pltpu.make_async_copy(w_hbm.at[pl.ds(b * FEAT, FEAT)], w.at[i], ld_sem.at[2 + i])
        copy.start()
        load_w.append(copy)

    sends = []

    def copy_to(src, dst, ss, rs, peer):
        return pltpu.make_async_remote_copy(
            src_ref=src, dst_ref=dst, send_sem=ss, recv_sem=rs, device_id=peer, device_id_type=MESH
        )

    def send(*args):
        copy = copy_to(*args)
        copy.start()
        sends.append(copy)
        return copy

    def pieces(n, body):
        if n == 1:
            body(0)
        else:
            pl.loop(0, n)(body)

    def grad_block(ph, s, block):
        span, width = spans[ph, s]
        half = core if block == 0 else 1 - core
        tile = 256 if width % 256 == 0 else width

        def body(j):
            cols = pl.ds(pl.multiple_of(span.start + j * tile, 128), tile)
            part = jnp.dot(xt[2 * ph + block], cot[:, cols], preferred_element_type=F32)
            g[ph, pl.ds(half * 2, 2), :, :, cols] = part.reshape(2, 8, 32, tile)

        pieces(width // tile, body)

    def input_block(i, write):
        load_w[i].wait()

        @pl.loop(0, 2)
        def _(j):
            rows = pl.ds(pl.multiple_of(j * 256, 256), 256)
            part = lax.dot_general(
                cot[...], w[i, rows, :], (((1,), (1,)), ((), ())), preferred_element_type=F32
            )
            write(rows, part)

    def rows_loop(body):
        @pl.loop(0, 16)
        def _(i):
            body(pl.ds(pl.multiple_of(i * 32, 32), 32))

    def view(stage, ph, s, to, i):
        cols = spans[ph, s][0]
        if stage == "ay":
            return ph, to, i, slice(None), cols
        if stage == "az":
            return ph, y, to, slice(None), cols
        if stage == "bz":
            return ph, i, to, slice(None), cols
        if stage[:2] == "hz":
            half = core if stage == "hz0" else 1 - core
            return ph, 2 * half + i, to, slice(None), cols
        return ph, to, z, slice(None), cols

    def ring(stage):
        n, count = RING[stage]
        return (n, count, y, y_peer) if stage[1] == "y" else (n, count, z, z_peer)

    def slot_of(n, way, k):
        return k if way > 0 else n // 2 + k - 1

    def came(stage, ph, s, way, k):
        n, _, _, peer = ring(stage)
        s_buf, r_buf, ss, rs = buffers[stage, ph, s]
        m = slot_of(n, way, k)
        copy_to(s_buf.at[m], r_buf.at[m], ss.at[m], rs.at[m], peer(way * turn)).wait_recv()
        return r_buf.at[m]

    def hop(stage, ph, s, way, k):
        n, count, place, peer = ring(stage)
        s_buf, r_buf, ss, rs = buffers[stage, ph, s]
        to = (place + n + way * turn * (n // 2 - k)) % n
        m = slot_of(n, way, k)
        first = k == (0 if way > 0 else 1)
        got = None if first else came(stage, ph, s, way, k - 1)

        def body(i):
            part = g[view(stage, ph, s, to, i)]
            if not first:
                part = part + decode(got[i])
            s_buf[m, i] = encode(part)

        pieces(count, body)
        if stage in LAST and k == n // 2 - 1:
            away = (mine + ph) % 2
            to_slot = m + away * ((n - 1 if way > 0 else n) - m)
            send(s_buf.at[m], r_buf.at[to_slot], ss.at[m], rs.at[to_slot], peer(way * turn, away))
        else:
            send(s_buf.at[m], r_buf.at[m], ss.at[m], rs.at[m], peer(way * turn))

    def finish(stage, ph, s):
        n, count, place, _ = ring(stage)
        last = [came(stage, ph, s, way, n // 2 - 1) for way in (1, -1)]

        def body(i):
            own = view(stage, ph, s, place, i)
            g[own] = g[own] + decode(last[0][i]) + decode(last[1][i])

        pieces(count, body)

    def own_part(stage, ph, s):
        n, _, place, _ = ring(stage)
        s_buf, r_buf, ss, rs = buffers[stage, ph, s]
        copy = copy_to(s_buf.at[n - 1], r_buf.at[n + 1], ss.at[n - 1], rs.at[n + 1], x_hi_peer)
        return view(stage, ph, s, place, 0), s_buf, copy

    def own_across(stage, ph, s):
        @pl.when(mine != ph)
        def _():
            own, s_buf, copy = own_part(stage, ph, s)
            s_buf[RING[stage][0] - 1, 0] = encode(g[own])
            copy.start()

    def last_finish(stage, ph, s):
        n, _, place, _ = ring(stage)
        s_buf, r_buf, ss, rs = buffers[stage, ph, s]

        @pl.when(mine == ph)
        def _():
            total = g[view(stage, ph, s, place, 0)]
            slots = (slot_of(n, 1, n // 2 - 1), slot_of(n, -1, n // 2 - 1), n - 1, n, n + 1)
            for m in slots:
                copy_to(s_buf.at[0], r_buf.at[m], ss.at[0], rs.at[m], x_hi_peer).wait_recv()
                total = total + decode(r_buf[m, 0])
            grad_out[:, spans[ph, s][0]] = total * norm

    def to_buffer(buf, k):
        def write(rows, part):
            buf[k, :, rows] = part

        return write

    flight = {}

    def send_features():
        flight["core"] = send(xt.at[0], xt.at[1], xt_ss.at[0], xt_rs.at[0], other_core)
        flight["chip"] = send(xt.at[0], xt.at[2], xt_ss.at[1], xt_rs.at[1], x_lo_peer)
        load_c.wait()

    def pass_features():
        flight["chip"].wait_recv()
        flight["pass"] = send(xt.at[2], xt.at[3], xt_ss.at[2], xt_rs.at[2], other_core)

    def partial_input_grad(i):
        input_block(i, to_buffer(pc_s if i % 2 == 0 else pp_s, i // 2))
        if i % 2 == 0:
            k = i // 2
            flight["pc", k] = send(pc_s.at[k], pc_r.at[k], pc_ss.at[k], pc_rs.at[k], other_core)

    def chip_sum():
        flight["pc", 0].wait_recv()

        def body(rows):
            pp_s[0, rows, :] = pp_s[0, rows, :] + pc_r[0, rows, :]

        rows_loop(body)
        flight["pp"] = send(pp_s.at[0], pp_r.at[0], pp_ss.at[0], pp_rs.at[0], x_lo_peer)

    def input_grad_sum():
        flight["pc", 1].wait_recv()
        flight["pp"].wait_recv()

        def body(rows):
            total = pp_s[1, rows, :] + pc_r[1, rows, :] + pp_r[0, rows, :]
            ig_out[rows, :] = total.astype(BF16)

        rows_loop(body)

    load_x.wait()
    xt[0] = (x_in[...] * jnp.array(LIFT, BF16)).T
    pl.semaphore_wait(barrier, len(partners))

    waits = {(0, 1): "core", (1, 1): "pass"}
    waited = set()
    for what, *at in ORDER:
        if what == "sendx":
            send_features()
        elif what == "fwd":
            pass_features()
        elif what[:2] == "ig":
            partial_input_grad(int(what[2]))
        elif what == "iadd":
            chip_sum()
        elif what == "ifin":
            input_grad_sum()
        elif what == "mg":
            ph, s, block = at
            key = waits.get((ph, block))
            if key and key not in waited:
                flight[key].wait_recv()
                waited.add(key)
            grad_block(ph, s, block)
        elif what == "xo":
            own_across(STAGES[STREAMS[at[0]][at[1]][0]][-1], *at)
        elif at[2] == "f":
            (last_finish if what in LAST else finish)(what, *at[:2])
        else:
            hop(what, at[0], at[1], 1 if at[2] == "m" else -1, at[3])
    for copy in sends:
        copy.wait_send()
    for ph, s, kind, *_ in streams():

        @pl.when(mine != ph)
        def _():
            own_part(STAGES[kind][-1], ph, s)[2].wait_send()


def reduce_all(norm, inputs, cotangent, weight):
    dma = pltpu.SemaphoreType.DMA
    nm = lambda *s: pltpu.VMEM(s, BF16)
    rings = []
    for _, _, kind, _, width in streams():
        for stage in STAGES[kind]:
            n, count = RING[stage]
            sent, came = (n, n + 2) if stage in LAST else (n - 1, n - 1)
            rings += [nm(sent, count, 32, width), nm(came, count, 32, width), dma((sent,)), dma((came,))]
    any_ = pl.BlockSpec(memory_space=pl.ANY)
    vm = pl.BlockSpec(memory_space=pltpu.VMEM)
    return pl.pallas_call(
        lambda *refs: kernel(norm, *refs),
        out_shape=(
            jax.ShapeDtypeStruct((32, COLS), F32),
            jax.ShapeDtypeStruct((TOK, FEAT), BF16),
        ),
        in_specs=[any_, any_, any_],
        out_specs=(vm, vm),
        scratch_shapes=[
            nm(TOK, FEAT), nm(4, FEAT, TOK), nm(TOK, COLS), nm(4, FEAT, COLS),
            pltpu.VMEM((2, 4, 8, 32, COLS), F32),
            pltpu.VMEM((2, TOK, FEAT), F32), pltpu.VMEM((2, TOK, FEAT), F32),
            pltpu.VMEM((2, TOK, FEAT), F32), pltpu.VMEM((1, TOK, FEAT), F32),
            dma((6,)), dma((3,)), dma((3,)),
            dma((2,)), dma((2,)), dma((1,)), dma((1,)),
            *rings,
        ],
        compiler_params=pltpu.CompilerParams(
            collective_id=1, has_side_effects=True, vmem_limit_bytes=60 * 2**20
        ),
        cost_estimate=pl.CostEstimate(flops=7516192768, bytes_accessed=12000000, transcendentals=0),
        name="reduce_all",
    )(inputs, cotangent, weight)


def update_kernel(grad, master, first, second, ig, new_master, new_first, new_second, ig_out):
    ig_out[...] = ig[...]
    out = adamw_update(grad[...], master[...], first[...], second[...])
    new_master[...], new_first[...], new_second[...] = out


def update(grad, master, first, second, input_grad):
    rows, tall = pl.BlockSpec((16, COLS), lambda i: (i, 0)), pl.BlockSpec((256, FEAT), lambda i: (i, 0))
    like = lambda a: jax.ShapeDtypeStruct(a.shape, a.dtype)
    return pl.pallas_call(
        update_kernel,
        out_shape=(like(master), like(first), like(second), like(input_grad)),
        grid=(2,),
        in_specs=[rows, rows, rows, rows, tall],
        out_specs=(rows, rows, rows, tall),
        name="update",
    )(grad, master, first, second, input_grad)


def local(inputs, cotangent, weight, master, first_moment, second_moment):
    token_count = inputs.shape[0]
    norm = float(lax.axis_size("dp") * token_count) ** (-0.5) / LIFT
    grad, input_grad = reduce_all(norm, inputs, cotangent, weight)
    out = update(grad, master, first_moment, second_moment, input_grad)
    new_master, new_first, new_second, input_grad = out
    return (input_grad, new_master, new_first, new_second)


def solution(mesh):
    split = P("dp", "fsdp")
    in_specs = (split, split, P(None, "fsdp"), split, split, split)
    return jax.shard_map(
        local, mesh=mesh, in_specs=in_specs, out_specs=(split,) * 4, check_vma=False
    )
```

```python
import jax
import jax.numpy as jnp
from jax import lax
from jax.experimental import pallas as pl
from jax.experimental.pallas import tpu as pltpu
from jax.sharding import PartitionSpec as P

MESH = pl.DeviceIdType.MESH
F32, BF16 = jnp.float32, jnp.bfloat16
TOK, FEAT, COLS = 512, 512, 1792
LIFT = 1024.0
STREAMS = (
    (("a", 512, "r"), ("a", 384, "r"), ("h", 896, "r")),
    (("a", 256, "t"), ("a", 512, "r"), ("a", 384, "t"), ("b", 128, "t"), ("b", 256, "t"), ("b", 256, "t")),
)
ORDER = (
    ("sendx",), ("ig0",), ("mg", 0, 1, 0), ("mg", 0, 0, 1), ("mg", 0, 1, 1), ("mg", 0, 2, 1),
    ("hz1", 0, 2, 0), ("mg", 0, 2, 0), ("ay", 0, 1, 0), ("hz0", 0, 2, 0), ("mg", 0, 0, 0), ("ay", 0, 0, 0),
    ("hz0", 0, 2, 4), ("hz1", 0, 2, 4), ("ay", 0, 1, 2), ("ig1",), ("iadd",), ("hz1", 0, 2, 1),
    ("ay", 0, 0, 2), ("hz0", 0, 2, 1), ("ig2",), ("ay", 0, 1, 1), ("hz0", 0, 2, 5), ("hz1", 0, 2, 5),
    ("ig3",), ("hz1", 0, 2, 2), ("fwd",), ("mg", 1, 0, 0), ("mg", 1, 1, 0), ("mg", 1, 2, 0),
    ("mg", 1, 5, 0), ("mg", 1, 4, 0), ("ay", 0, 0, 1), ("mg", 1, 1, 1), ("ay", 1, 1, 0), ("ay", 1, 1, 2),
    ("mg", 1, 4, 1), ("bz", 1, 4, 4), ("bz", 1, 4, 0), ("mg", 1, 5, 1), ("mg", 1, 2, 1), ("mg", 1, 0, 1),
    ("ay", 1, 0, 0), ("bz", 1, 5, 0), ("ay", 1, 2, 0), ("hz0", 0, 2, 2), ("bz", 1, 5, 4), ("mg", 1, 3, 1),
    ("ay", 1, 0, 2), ("mg", 1, 3, 0), ("bz", 1, 3, 0), ("ay", 0, 1, "f"), ("az", 0, 1, 0), ("hz0", 0, 2, 6),
    ("ay", 1, 2, 2), ("hz1", 0, 2, 6), ("bz", 1, 4, 5), ("bz", 1, 4, 1), ("hz1", 0, 2, 3), ("bz", 1, 3, 4),
    ("az", 0, 1, 4), ("xo", 0, 1), ("bz", 1, 5, 1), ("bz", 1, 5, 5), ("ay", 0, 0, "f"), ("az", 0, 0, 0),
    ("az", 0, 0, 4), ("hz0", 0, 2, 3), ("xo", 0, 0), ("bz", 1, 3, 1), ("az", 0, 1, 1), ("bz", 1, 4, 2),
    ("ay", 1, 1, 1), ("bz", 1, 4, 6), ("hz1", 0, 2, "f"), ("bz", 1, 3, 5), ("bz", 1, 5, 2), ("az", 0, 1, 5),
    ("az", 0, 0, 1), ("ay", 1, 0, 1), ("bz", 1, 5, 6), ("az", 0, 0, 5), ("hz0", 0, 2, "f"), ("ay", 1, 2, 1),
    ("by", 0, 2, 0), ("xo", 0, 2), ("bz", 1, 3, 2), ("by", 0, 2, 2), ("bz", 1, 3, 6), ("az", 0, 1, 2),
    ("az", 0, 1, 6), ("bz", 1, 4, 3), ("ay", 1, 1, "f"), ("az", 1, 1, 4), ("az", 1, 1, 0), ("xo", 1, 1),
    ("az", 0, 0, 6), ("bz", 1, 5, 3), ("az", 0, 0, 2), ("ay", 1, 0, "f"), ("xo", 1, 0), ("az", 1, 0, 2),
    ("bz", 1, 3, 3), ("az", 1, 0, 0), ("az", 1, 0, 3), ("az", 1, 0, 4), ("az", 0, 1, 3), ("az", 1, 0, 1),
    ("bz", 1, 4, "f"), ("xo", 1, 4), ("by", 1, 4, 0), ("by", 1, 4, 1), ("by", 1, 4, 2), ("az", 1, 1, 5),
    ("az", 1, 1, 1), ("ay", 1, 2, "f"), ("az", 1, 2, 1), ("az", 1, 2, 0), ("by", 0, 2, 1), ("xo", 1, 2),
    ("az", 1, 2, 3), ("bz", 1, 5, "f"), ("by", 1, 5, 1), ("by", 1, 5, 0), ("az", 1, 2, 4), ("xo", 1, 5),
    ("az", 0, 0, 3), ("by", 1, 5, 2), ("az", 1, 2, 2), ("az", 1, 0, 6), ("bz", 1, 3, "f"), ("xo", 1, 3),
    ("by", 1, 3, 2), ("by", 1, 3, 1), ("by", 1, 3, 0), ("az", 1, 0, 5), ("az", 1, 1, 6), ("az", 0, 1, "f"),
    ("az", 1, 1, 2), ("by", 1, 4, "f"), ("by", 0, 2, "f"), ("az", 1, 2, 5), ("az", 1, 2, 6),
    ("az", 0, 0, "f"), ("ifin",), ("az", 1, 1, 3), ("az", 1, 0, "f"), ("by", 1, 5, "f"), ("by", 1, 3, "f"),
    ("az", 1, 2, "f"), ("az", 1, 1, "f"),
)


def encode(x):
    s = x * x
    return (s * (x * jnp.abs(x))).astype(BF16)


def decode(c):
    c = c.astype(F32)
    t = lax.rsqrt(lax.rsqrt(jnp.abs(c)))
    return jnp.where(c < 0, -t, t)


def adamw_update(grad, master, first_moment, second_moment):
    new_first = 0.9 * first_moment + 0.1 * grad
    new_second = 0.95 * second_moment + 0.05 * grad * grad
    corrected = new_first / (1.0 - 0.9**10) / (jnp.sqrt(new_second / (1.0 - 0.95**10)) + 1e-08)
    new_master = master - 0.001 * (corrected + 0.1 * master)
    return (new_master, new_first, new_second)


STAGES = {"a": ("ay", "az"), "b": ("bz", "by"), "h": ("hz0", "hz1", "by")}
COUNT = {"ay": 8, "az": 1, "bz": 4, "hz0": 2, "hz1": 2, "by": 1}
LAST = ("az", "by")
PLANS = {
    "yr": ((2, 1, ()), (1, 1, (0,)), (-1, -1, ())),
    "yt": ((2, 2, ()), (1, 1, ()), (-1, -1, ())),
    "zr": ((4, 1, ()), (3, 1, (0,)), (2, 1, (1,)), (1, 1, (2,)), (-3, -1, ()), (-2, -1, (4,)), (-1, -1, (5,))),
    "zt": ((4, 2, ()), (3, 1, ()), (-3, -1, ()), (1, 1, ()), (-1, -1, ()), (2, 2, (0, 1)), (-2, -2, (2,))),
}


def plan_of(stage, way):
    return PLANS[("y" if stage[1] == "y" else "z") + (way if stage in LAST else "r")]


def ends_of(plan):
    return [i for i, (owner, to, _) in enumerate(plan) if owner == to]


def streams():
    for ph, cut in enumerate(STREAMS):
        first = 0
        for s, (kind, width, way) in enumerate(cut):
            yield ph, s, kind, first, width, way
            first += width


def kernel(norm, x_hbm, c_hbm, w_hbm, grad_out, ig_out, *scratch):
    x_in, xt, cot, w, g, pc_s, pc_r, pp_s, pp_r = scratch[:9]
    ld_sem, xt_ss, xt_rs, pc_ss, pc_rs, pp_ss, pp_rs = scratch[9:16]
    rest = list(scratch[16:])
    buffers = {}
    spans = {}
    for ph, s, kind, first, width, way in streams():
        spans[ph, s] = pl.ds(first, width), width, way
        for stage in STAGES[kind]:
            buffers[stage, ph, s], rest = rest[:4], rest[4:]

    f, d = lax.axis_index("fsdp"), lax.axis_index("dp")
    x_lo, core = f // 2, f % 2
    x_hi, y, z = d // 32, (d // 8) % 4, d % 8
    turn = 1 - 2 * core
    mine = (x_lo + x_hi) % 2
    other_core = {"dp": d, "fsdp": x_lo * 2 + (1 - core)}
    x_lo_peer = {"dp": d, "fsdp": (1 - x_lo) * 2 + core}
    x_hi_peer = {"dp": (1 - x_hi) * 32 + y * 8 + z, "fsdp": f}

    y_at = {k: (y + 4 + turn * k) % 4 for k in range(-2, 3)}
    z_at = {k: (z + 8 + turn * k) % 8 for k in range(-4, 5)}
    away = {ph: (mine + ph) % 2 for ph in (0, 1)}
    sides = {None: x_hi, 0: (x_lo + 0) % 2, 1: (x_lo + 1) % 2, "x": 1 - x_hi}
    y_dev = {(k, s): {"dp": x * 32 + y_at[k] * 8 + z, "fsdp": f} for k in (-2, -1, 1, 2) for s, x in sides.items()}
    z_dev = {(k, s): {"dp": x * 32 + y * 8 + z_at[k], "fsdp": f} for k in (-2, -1, 1, 2) for s, x in sides.items()}

    barrier = pltpu.get_barrier_semaphore()
    partners = [other_core, x_lo_peer, x_hi_peer]
    far = {"y": 1, "z": 1}
    for _, _, kind, _, _, way in streams():
        last = STAGES[kind][-1]
        far[last[1]] = max(far[last[1]], *(to for _, to, _ in plan_of(last, way)))
    for dev, reach in ((y_dev, far["y"]), (z_dev, far["z"])):
        steps = [k for k in (1, -1, 2, -2) if abs(k) <= reach and (dev is z_dev or k != -2)]
        partners += [dev[k, side] for k in steps for side in (None, "x")]
    load_x = pltpu.make_async_copy(x_hbm, x_in, ld_sem.at[0])
    load_x.start()
    load_c = pltpu.make_async_copy(c_hbm, cot, ld_sem.at[1])
    load_c.start()
    for p in partners:
        pl.semaphore_signal(barrier, inc=1, device_id=p, device_id_type=MESH)
    blocks = ((1 - x_lo) * 2 + (1 - core), (1 - x_lo) * 2 + core, x_lo * 2 + (1 - core), f)
    load_w = []
    for i, b in enumerate(blocks):
        copy = pltpu.make_async_copy(w_hbm.at[pl.ds(b * FEAT, FEAT)], w.at[i], ld_sem.at[2 + i])
        copy.start()
        load_w.append(copy)

    sends = []

    def copy_to(src, dst, ss, rs, peer):
        return pltpu.make_async_remote_copy(
            src_ref=src, dst_ref=dst, send_sem=ss, recv_sem=rs, device_id=peer, device_id_type=MESH
        )

    def send(*args):
        copy = copy_to(*args)
        copy.start()
        sends.append(copy)
        return copy

    def pieces(n, body):
        if n == 1:
            body(0)
        else:
            pl.loop(0, n)(body)

    def grad_block(ph, s, block):
        span, width, _ = spans[ph, s]
        half = core if block == 0 else 1 - core
        tile = 256 if width % 256 == 0 else width

        def body(j):
            cols = pl.ds(pl.multiple_of(span.start + j * tile, 128), tile)
            part = jnp.dot(xt[2 * ph + block], cot[:, cols], preferred_element_type=F32)
            g[ph, pl.ds(half * 2, 2), :, :, cols] = part.reshape(2, 8, 32, tile)

        pieces(width // tile, body)

    def input_block(i, write):
        load_w[i].wait()

        @pl.loop(0, 2)
        def _(j):
            rows = pl.ds(pl.multiple_of(j * 256, 256), 256)
            part = lax.dot_general(
                cot[...], w[i, rows, :], (((1,), (1,)), ((), ())), preferred_element_type=F32
            )
            write(rows, part)

    def rows_loop(body):
        @pl.loop(0, 16)
        def _(i):
            body(pl.ds(pl.multiple_of(i * 32, 32), 32))

    def view(stage, ph, s, to, i):
        cols = spans[ph, s][0]
        if stage == "ay":
            return ph, to, i, slice(None), cols
        if stage == "az":
            return ph, y, to, slice(None), cols
        if stage == "bz":
            return ph, i, to, slice(None), cols
        if stage[:2] == "hz":
            half = core if stage == "hz0" else 1 - core
            return ph, 2 * half + i, to, slice(None), cols
        return ph, to, z, slice(None), cols

    def ring(stage):
        return (y_at, y_dev) if stage[1] == "y" else (z_at, z_dev)

    def came(stage, ph, s, m):
        s_buf, r_buf, ss, rs = buffers[stage, ph, s]
        copy_to(s_buf.at[0], r_buf.at[m], ss.at[0], rs.at[m], x_hi_peer).wait_recv()
        return r_buf.at[m]

    ready = set()

    def message(stage, ph, s, m, only_encode=False):
        places, devices = ring(stage)
        s_buf, r_buf, ss, rs = buffers[stage, ph, s]
        plan = plan_of(stage, spans[ph, s][2])
        owner, to, joins = plan[m]
        chunk = places[owner]
        got = [came(stage, ph, s, i) for i in joins]

        def body(i):
            part = g[view(stage, ph, s, chunk, i)]
            for other in got:
                part = part + decode(other[i])
            s_buf[m, i] = encode(part)

        if (stage, ph, s, m) not in ready:
            pieces(COUNT[stage], body)
        if only_encode:
            ready.add((stage, ph, s, m))
            return
        if stage in LAST and owner == to:
            slot = m + away[ph] * (len(plan) + ends_of(plan).index(m) - m)
            send(s_buf.at[m], r_buf.at[slot], ss.at[m], rs.at[slot], devices[to, ph])
        else:
            send(s_buf.at[m], r_buf.at[m], ss.at[m], rs.at[m], devices[to, None])

    def finish(stage, ph, s):
        place = ring(stage)[0][0]
        plan = plan_of(stage, spans[ph, s][2])
        last = [came(stage, ph, s, m) for m in ends_of(plan)]

        def body(i):
            own = view(stage, ph, s, place, i)
            g[own] = g[own] + decode(last[0][i]) + decode(last[1][i])

        pieces(COUNT[stage], body)

    def own_part(stage, ph, s):
        place = ring(stage)[0][0]
        s_buf, r_buf, ss, rs = buffers[stage, ph, s]
        plan = plan_of(stage, spans[ph, s][2])
        m, slot = len(plan), len(plan) + len(ends_of(plan))
        copy = copy_to(s_buf.at[m], r_buf.at[slot], ss.at[m], rs.at[slot], x_hi_peer)
        return view(stage, ph, s, place, 0), s_buf.at[m], copy

    def own_across(stage, ph, s):
        @pl.when(mine != ph)
        def _():
            own, buffer, copy = own_part(stage, ph, s)
            buffer[0] = encode(g[own])
            copy.start()

    def last_finish(stage, ph, s):
        plan = plan_of(stage, spans[ph, s][2])
        ends = ends_of(plan)

        @pl.when(mine == ph)
        def _():
            total = g[view(stage, ph, s, ring(stage)[0][0], 0)]
            for m in ends + [len(plan) + i for i in range(len(ends) + 1)]:
                total = total + decode(came(stage, ph, s, m)[0])
            grad_out[:, spans[ph, s][0]] = total * norm

    def to_buffer(buf, k):
        def write(rows, part):
            buf[k, :, rows] = part

        return write

    flight = {}

    def send_features():
        flight["core"] = send(xt.at[0], xt.at[1], xt_ss.at[0], xt_rs.at[0], other_core)
        flight["chip"] = send(xt.at[0], xt.at[2], xt_ss.at[1], xt_rs.at[1], x_lo_peer)

    def pass_features():
        flight["chip"].wait_recv()
        flight["pass"] = send(xt.at[2], xt.at[3], xt_ss.at[2], xt_rs.at[2], other_core)

    def partial_input_grad(i):
        input_block(i, to_buffer(pc_s if i % 2 == 0 else pp_s, i // 2))
        if i % 2 == 0:
            k = i // 2
            flight["pc", k] = send(pc_s.at[k], pc_r.at[k], pc_ss.at[k], pc_rs.at[k], other_core)

    def chip_sum():
        flight["pc", 0].wait_recv()

        def body(rows):
            pp_s[0, rows, :] = pp_s[0, rows, :] + pc_r[0, rows, :]

        rows_loop(body)
        flight["pp"] = send(pp_s.at[0], pp_r.at[0], pp_ss.at[0], pp_rs.at[0], x_lo_peer)

    def input_grad_sum():
        flight["pc", 1].wait_recv()
        flight["pp"].wait_recv()

        def body(rows):
            total = pp_s[1, rows, :] + pc_r[1, rows, :] + pp_r[0, rows, :]
            ig_out[rows, :] = total.astype(BF16)

        rows_loop(body)

    load_x.wait()
    xt[0] = (x_in[...] * jnp.array(LIFT, BF16)).T
    load_c.wait()
    first = [at for at in ORDER if at[0] == "mg" and at[1] == at[3] == 0]
    for at in first:
        grad_block(*at[1:])
    for stage, *at in ORDER:
        if stage == "hz0" and at[0] == 0 and at[2] != "f":
            if not plan_of(stage, "r")[at[2]][2]:
                message(stage, *at, only_encode=True)
    pl.semaphore_wait(barrier, len(partners))

    waits = {(0, 1): "core", (1, 1): "pass"}
    waited = set()
    for what, *at in ORDER:
        if what == "sendx":
            send_features()
        elif what == "fwd":
            pass_features()
        elif what[:2] == "ig":
            partial_input_grad(int(what[2]))
        elif what == "iadd":
            chip_sum()
        elif what == "ifin":
            input_grad_sum()
        elif what == "mg":
            ph, s, block = at
            if ph == block == 0:
                continue
            key = waits.get((ph, block))
            if key and key not in waited:
                flight[key].wait_recv()
                waited.add(key)
            grad_block(ph, s, block)
        elif what == "xo":
            own_across(STAGES[STREAMS[at[0]][at[1]][0]][-1], *at)
        elif at[2] == "f":
            (last_finish if what in LAST else finish)(what, *at[:2])
        else:
            message(what, *at)
    for copy in sends:
        copy.wait_send()
    for ph, s, kind, *_ in streams():

        @pl.when(mine != ph)
        def _():
            own_part(STAGES[kind][-1], ph, s)[2].wait_send()


def reduce_all(norm, inputs, cotangent, weight):
    dma = pltpu.SemaphoreType.DMA
    nm = lambda *s: pltpu.VMEM(s, BF16)
    rings = []
    for _, _, kind, _, width, way in streams():
        for stage in STAGES[kind]:
            plan, count = plan_of(stage, way), COUNT[stage]
            sent = came = len(plan)
            if stage in LAST:
                sent, came = sent + 1, came + len(ends_of(plan)) + 1
            rings += [nm(sent, count, 32, width), nm(came, count, 32, width), dma((sent,)), dma((came,))]
    any_ = pl.BlockSpec(memory_space=pl.ANY)
    vm = pl.BlockSpec(memory_space=pltpu.VMEM)
    return pl.pallas_call(
        lambda *refs: kernel(norm, *refs),
        out_shape=(
            jax.ShapeDtypeStruct((32, COLS), F32),
            jax.ShapeDtypeStruct((TOK, FEAT), BF16),
        ),
        in_specs=[any_, any_, any_],
        out_specs=(vm, vm),
        scratch_shapes=[
            nm(TOK, FEAT), nm(4, FEAT, TOK), nm(TOK, COLS), nm(4, FEAT, COLS),
            pltpu.VMEM((2, 4, 8, 32, COLS), F32),
            pltpu.VMEM((2, TOK, FEAT), F32), pltpu.VMEM((2, TOK, FEAT), F32),
            pltpu.VMEM((2, TOK, FEAT), F32), pltpu.VMEM((1, TOK, FEAT), F32),
            dma((6,)), dma((3,)), dma((3,)),
            dma((2,)), dma((2,)), dma((1,)), dma((1,)),
            *rings,
        ],
        compiler_params=pltpu.CompilerParams(
            collective_id=1, has_side_effects=True, vmem_limit_bytes=60 * 2**20
        ),
        cost_estimate=pl.CostEstimate(flops=7516192768, bytes_accessed=12000000, transcendentals=0),
        name="reduce_all",
    )(inputs, cotangent, weight)


def update_kernel(grad, master, first, second, ig, new_master, new_first, new_second, ig_out):
    ig_out[...] = ig[...]
    out = adamw_update(grad[...], master[...], first[...], second[...])
    new_master[...], new_first[...], new_second[...] = out


def update(grad, master, first, second, input_grad):
    rows, tall = pl.BlockSpec((16, COLS), lambda i: (i, 0)), pl.BlockSpec((256, FEAT), lambda i: (i, 0))
    like = lambda a: jax.ShapeDtypeStruct(a.shape, a.dtype)
    return pl.pallas_call(
        update_kernel,
        out_shape=(like(master), like(first), like(second), like(input_grad)),
        grid=(2,),
        in_specs=[rows, rows, rows, rows, tall],
        out_specs=(rows, rows, rows, tall),
        name="update",
    )(grad, master, first, second, input_grad)


def local(inputs, cotangent, weight, master, first_moment, second_moment):
    token_count = inputs.shape[0]
    norm = float(lax.axis_size("dp") * token_count) ** (-0.5) / LIFT
    grad, input_grad = reduce_all(norm, inputs, cotangent, weight)
    out = update(grad, master, first_moment, second_moment, input_grad)
    new_master, new_first, new_second, input_grad = out
    return (input_grad, new_master, new_first, new_second)


def solution(mesh):
    split = P("dp", "fsdp")
    in_specs = (split, split, P(None, "fsdp"), split, split, split)
    return jax.shard_map(
        local, mesh=mesh, in_specs=in_specs, out_specs=(split,) * 4, check_vma=False
    )
```

```python
import jax
import jax.numpy as jnp
from jax import lax
from jax.experimental import pallas as pl
from jax.experimental.pallas import tpu as pltpu
from jax.sharding import PartitionSpec as P

MESH = pl.DeviceIdType.MESH
F32, BF16 = jnp.float32, jnp.bfloat16
TOK, FEAT, COLS = 512, 512, 1792
LIFT = 1024.0
STREAMS = (
    (("a", 512, "r"), ("a", 384, "r"), ("h", 896, "r")),
    (("a", 256, "t"), ("a", 512, "r"), ("a", 384, "t"), ("b", 128, "t"), ("b", 256, "t"), ("b", 256, "t")),
)
ORDER = (
    ("sendx",), ("ig0",), ("mg", 0, 1, 0), ("mg", 0, 0, 1), ("mg", 0, 1, 1), ("mg", 0, 2, 1),
    ("hz1", 0, 2, 0), ("mg", 0, 2, 0), ("ay", 0, 1, 0), ("hz0", 0, 2, 0), ("mg", 0, 0, 0), ("ay", 0, 0, 0),
    ("hz0", 0, 2, 4), ("hz1", 0, 2, 4), ("ay", 0, 1, 2), ("ig1",), ("iadd",), ("hz1", 0, 2, 1),
    ("ay", 0, 0, 2), ("hz0", 0, 2, 1), ("ig2",), ("ay", 0, 1, 1), ("hz0", 0, 2, 5), ("hz1", 0, 2, 5),
    ("ig3",), ("hz1", 0, 2, 2), ("fwd",), ("mg", 1, 0, 0), ("mg", 1, 1, 0), ("mg", 1, 2, 0),
    ("mg", 1, 5, 0), ("mg", 1, 4, 0), ("ay", 0, 0, 1), ("mg", 1, 1, 1), ("ay", 1, 1, 0), ("ay", 1, 1, 2),
    ("mg", 1, 4, 1), ("bz", 1, 4, 4), ("bz", 1, 4, 0), ("mg", 1, 5, 1), ("mg", 1, 2, 1), ("mg", 1, 0, 1),
    ("ay", 1, 0, 0), ("bz", 1, 5, 0), ("ay", 1, 2, 0), ("hz0", 0, 2, 2), ("bz", 1, 5, 4), ("mg", 1, 3, 1),
    ("ay", 1, 0, 2), ("mg", 1, 3, 0), ("bz", 1, 3, 0), ("ay", 0, 1, "f"), ("az", 0, 1, 0), ("hz0", 0, 2, 6),
    ("ay", 1, 2, 2), ("hz1", 0, 2, 6), ("bz", 1, 4, 5), ("bz", 1, 4, 1), ("hz1", 0, 2, 3), ("bz", 1, 3, 4),
    ("az", 0, 1, 4), ("xo", 0, 1), ("bz", 1, 5, 1), ("bz", 1, 5, 5), ("ay", 0, 0, "f"), ("az", 0, 0, 0),
    ("az", 0, 0, 4), ("hz0", 0, 2, 3), ("xo", 0, 0), ("bz", 1, 3, 1), ("az", 0, 1, 1), ("bz", 1, 4, 2),
    ("ay", 1, 1, 1), ("bz", 1, 4, 6), ("hz1", 0, 2, "f"), ("bz", 1, 3, 5), ("bz", 1, 5, 2), ("az", 0, 1, 5),
    ("az", 0, 0, 1), ("ay", 1, 0, 1), ("bz", 1, 5, 6), ("az", 0, 0, 5), ("hz0", 0, 2, "f"), ("ay", 1, 2, 1),
    ("by", 0, 2, 0), ("xo", 0, 2), ("bz", 1, 3, 2), ("by", 0, 2, 2), ("bz", 1, 3, 6), ("az", 0, 1, 2),
    ("az", 0, 1, 6), ("bz", 1, 4, 3), ("ay", 1, 1, "f"), ("az", 1, 1, 4), ("az", 1, 1, 0), ("xo", 1, 1),
    ("az", 0, 0, 6), ("bz", 1, 5, 3), ("az", 0, 0, 2), ("ay", 1, 0, "f"), ("xo", 1, 0), ("az", 1, 0, 2),
    ("bz", 1, 3, 3), ("az", 1, 0, 0), ("az", 1, 0, 3), ("az", 1, 0, 4), ("az", 0, 1, 3), ("az", 1, 0, 1),
    ("bz", 1, 4, "f"), ("xo", 1, 4), ("by", 1, 4, 0), ("by", 1, 4, 1), ("by", 1, 4, 2), ("az", 1, 1, 5),
    ("az", 1, 1, 1), ("ay", 1, 2, "f"), ("az", 1, 2, 1), ("az", 1, 2, 0), ("by", 0, 2, 1), ("xo", 1, 2),
    ("az", 1, 2, 3), ("bz", 1, 5, "f"), ("by", 1, 5, 1), ("by", 1, 5, 0), ("az", 1, 2, 4), ("xo", 1, 5),
    ("az", 0, 0, 3), ("by", 1, 5, 2), ("az", 1, 2, 2), ("az", 1, 0, 6), ("bz", 1, 3, "f"), ("xo", 1, 3),
    ("by", 1, 3, 2), ("by", 1, 3, 1), ("by", 1, 3, 0), ("az", 1, 0, 5), ("az", 1, 1, 6), ("az", 0, 1, "f"),
    ("az", 1, 1, 2), ("by", 1, 4, "f"), ("by", 0, 2, "f"), ("az", 1, 2, 5), ("az", 1, 2, 6),
    ("az", 0, 0, "f"), ("ifin",), ("az", 1, 1, 3), ("az", 1, 0, "f"), ("by", 1, 5, "f"), ("by", 1, 3, "f"),
    ("az", 1, 2, "f"), ("az", 1, 1, "f"),
)


def encode(x):
    s = x * x
    return (s * (x * jnp.abs(x))).astype(BF16)


def decode(c):
    c = c.astype(F32)
    t = lax.rsqrt(lax.rsqrt(jnp.abs(c)))
    return jnp.where(c < 0, -t, t)


def adamw_update(grad, master, first_moment, second_moment):
    new_first = 0.9 * first_moment + 0.1 * grad
    new_second = 0.95 * second_moment + 0.05 * grad * grad
    corrected = new_first / (1.0 - 0.9**10) / (jnp.sqrt(new_second / (1.0 - 0.95**10)) + 1e-08)
    new_master = master - 0.001 * (corrected + 0.1 * master)
    return (new_master, new_first, new_second)


STAGES = {"a": ("ay", "az"), "b": ("bz", "by"), "h": ("hz0", "hz1", "by")}
COUNT = {"ay": 8, "az": 1, "bz": 4, "hz0": 2, "hz1": 2, "by": 1}
LAST = ("az", "by")
PLANS = {
    "yr": ((2, 1, ()), (1, 1, (0,)), (-1, -1, ())),
    "yt": ((2, 2, ()), (1, 1, ()), (-1, -1, ())),
    "zr": ((4, 1, ()), (3, 1, (0,)), (2, 1, (1,)), (1, 1, (2,)), (-3, -1, ()), (-2, -1, (4,)), (-1, -1, (5,))),
    "zt": ((4, 2, ()), (3, 1, ()), (-3, -1, ()), (1, 1, ()), (-1, -1, ()), (2, 2, (0, 1)), (-2, -2, (2,))),
}


def plan_of(stage, way):
    return PLANS[("y" if stage[1] == "y" else "z") + (way if stage in LAST else "r")]


def ends_of(plan):
    return [i for i, (owner, to, _) in enumerate(plan) if owner == to]


def streams():
    for ph, cut in enumerate(STREAMS):
        first = 0
        for s, (kind, width, way) in enumerate(cut):
            yield ph, s, kind, first, width, way
            first += width


def kernel(norm, x_hbm, c_hbm, w_hbm, grad_out, ig_out, *scratch):
    x_in, xt, cot, w, g, pc_s, pc_r, pp_s, pp_r = scratch[:9]
    ld_sem, xt_ss, xt_rs, pc_ss, pc_rs, pp_ss, pp_rs = scratch[9:16]
    rest = list(scratch[16:-2])
    ig_buf, ig_sem = scratch[-2:]
    write_ig = pltpu.make_async_copy(ig_buf, ig_out, ig_sem)
    buffers = {}
    spans = {}
    for ph, s, kind, first, width, way in streams():
        spans[ph, s] = pl.ds(first, width), width, way
        for stage in STAGES[kind]:
            buffers[stage, ph, s], rest = rest[:4], rest[4:]

    f, d = lax.axis_index("fsdp"), lax.axis_index("dp")
    x_lo, core = f // 2, f % 2
    x_hi, y, z = d // 32, (d // 8) % 4, d % 8
    turn = 1 - 2 * core
    mine = (x_lo + x_hi) % 2
    other_core = {"dp": d, "fsdp": x_lo * 2 + (1 - core)}
    x_lo_peer = {"dp": d, "fsdp": (1 - x_lo) * 2 + core}
    x_hi_peer = {"dp": (1 - x_hi) * 32 + y * 8 + z, "fsdp": f}

    y_at = {k: (y + 4 + turn * k) % 4 for k in range(-2, 3)}
    z_at = {k: (z + 8 + turn * k) % 8 for k in range(-4, 5)}
    away = {ph: (mine + ph) % 2 for ph in (0, 1)}
    sides = {None: x_hi, 0: (x_lo + 0) % 2, 1: (x_lo + 1) % 2, "x": 1 - x_hi}
    y_dev = {(k, s): {"dp": x * 32 + y_at[k] * 8 + z, "fsdp": f} for k in (-2, -1, 1, 2) for s, x in sides.items()}
    z_dev = {(k, s): {"dp": x * 32 + y * 8 + z_at[k], "fsdp": f} for k in (-2, -1, 1, 2) for s, x in sides.items()}

    barrier = pltpu.get_barrier_semaphore()
    partners = [other_core, x_lo_peer, x_hi_peer]
    far = {"y": 1, "z": 1}
    for _, _, kind, _, _, way in streams():
        last = STAGES[kind][-1]
        far[last[1]] = max(far[last[1]], *(to for _, to, _ in plan_of(last, way)))
    for dev, reach in ((y_dev, far["y"]), (z_dev, far["z"])):
        steps = [k for k in (1, -1, 2, -2) if abs(k) <= reach and (dev is z_dev or k != -2)]
        partners += [dev[k, side] for k in steps for side in (None, "x")]
    load_x = pltpu.make_async_copy(x_hbm, x_in, ld_sem.at[0])
    load_x.start()
    load_c = pltpu.make_async_copy(c_hbm, cot, ld_sem.at[1])
    load_c.start()
    for p in partners:
        pl.semaphore_signal(barrier, inc=1, device_id=p, device_id_type=MESH)
    blocks = ((1 - x_lo) * 2 + (1 - core), (1 - x_lo) * 2 + core, x_lo * 2 + (1 - core), f)
    load_w = []
    for i, b in enumerate(blocks):
        copy = pltpu.make_async_copy(w_hbm.at[pl.ds(b * FEAT, FEAT)], w.at[i], ld_sem.at[2 + i])
        copy.start()
        load_w.append(copy)

    sends = []

    def copy_to(src, dst, ss, rs, peer):
        return pltpu.make_async_remote_copy(
            src_ref=src, dst_ref=dst, send_sem=ss, recv_sem=rs, device_id=peer, device_id_type=MESH
        )

    def send(*args):
        copy = copy_to(*args)
        copy.start()
        sends.append(copy)
        return copy

    def pieces(n, body):
        if n == 1:
            body(0)
        else:
            pl.loop(0, n)(body)

    def grad_block(ph, s, block):
        span, width, _ = spans[ph, s]
        half = core if block == 0 else 1 - core
        tile = 256 if width % 256 == 0 else width

        def body(j):
            cols = pl.ds(pl.multiple_of(span.start + j * tile, 128), tile)
            part = jnp.dot(xt[2 * ph + block], cot[:, cols], preferred_element_type=F32)
            g[ph, pl.ds(half * 2, 2), :, :, cols] = part.reshape(2, 8, 32, tile)

        pieces(width // tile, body)

    def input_block(i, write):
        load_w[i].wait()

        @pl.loop(0, 2)
        def _(j):
            rows = pl.ds(pl.multiple_of(j * 256, 256), 256)
            part = lax.dot_general(
                cot[...], w[i, rows, :], (((1,), (1,)), ((), ())), preferred_element_type=F32
            )
            write(rows, part)

    def rows_loop(body):
        @pl.loop(0, 16)
        def _(i):
            body(pl.ds(pl.multiple_of(i * 32, 32), 32))

    def view(stage, ph, s, to, i):
        cols = spans[ph, s][0]
        if stage == "ay":
            return ph, to, i, slice(None), cols
        if stage == "az":
            return ph, y, to, slice(None), cols
        if stage == "bz":
            return ph, i, to, slice(None), cols
        if stage[:2] == "hz":
            half = core if stage == "hz0" else 1 - core
            return ph, 2 * half + i, to, slice(None), cols
        return ph, to, z, slice(None), cols

    def ring(stage):
        return (y_at, y_dev) if stage[1] == "y" else (z_at, z_dev)

    def came(stage, ph, s, m):
        s_buf, r_buf, ss, rs = buffers[stage, ph, s]
        copy_to(s_buf.at[0], r_buf.at[m], ss.at[0], rs.at[m], x_hi_peer).wait_recv()
        return r_buf.at[m]

    ready = set()

    def message(stage, ph, s, m, only_encode=False):
        places, devices = ring(stage)
        s_buf, r_buf, ss, rs = buffers[stage, ph, s]
        plan = plan_of(stage, spans[ph, s][2])
        owner, to, joins = plan[m]
        chunk = places[owner]
        got = [came(stage, ph, s, i) for i in joins]

        def body(i):
            part = g[view(stage, ph, s, chunk, i)]
            for other in got:
                part = part + decode(other[i])
            s_buf[m, i] = encode(part)

        if (stage, ph, s, m) not in ready:
            pieces(COUNT[stage], body)
        if only_encode:
            ready.add((stage, ph, s, m))
            return
        if stage in LAST and owner == to:
            slot = m + away[ph] * (len(plan) + ends_of(plan).index(m) - m)
            send(s_buf.at[m], r_buf.at[slot], ss.at[m], rs.at[slot], devices[to, ph])
        else:
            send(s_buf.at[m], r_buf.at[m], ss.at[m], rs.at[m], devices[to, None])

    def finish(stage, ph, s):
        place = ring(stage)[0][0]
        plan = plan_of(stage, spans[ph, s][2])
        last = [came(stage, ph, s, m) for m in ends_of(plan)]

        def body(i):
            own = view(stage, ph, s, place, i)
            g[own] = g[own] + decode(last[0][i]) + decode(last[1][i])

        pieces(COUNT[stage], body)

    def own_part(stage, ph, s):
        place = ring(stage)[0][0]
        s_buf, r_buf, ss, rs = buffers[stage, ph, s]
        plan = plan_of(stage, spans[ph, s][2])
        m, slot = len(plan), len(plan) + len(ends_of(plan))
        copy = copy_to(s_buf.at[m], r_buf.at[slot], ss.at[m], rs.at[slot], x_hi_peer)
        return view(stage, ph, s, place, 0), s_buf.at[m], copy

    def own_across(stage, ph, s):
        @pl.when(mine != ph)
        def _():
            own, buffer, copy = own_part(stage, ph, s)
            buffer[0] = encode(g[own])
            copy.start()

    def last_finish(stage, ph, s):
        plan = plan_of(stage, spans[ph, s][2])
        ends = ends_of(plan)

        @pl.when(mine == ph)
        def _():
            total = g[view(stage, ph, s, ring(stage)[0][0], 0)]
            for m in ends + [len(plan) + i for i in range(len(ends) + 1)]:
                total = total + decode(came(stage, ph, s, m)[0])
            grad_out[:, spans[ph, s][0]] = total * norm

    def to_buffer(buf, k):
        def write(rows, part):
            buf[k, :, rows] = part

        return write

    flight = {}

    def send_features():
        flight["core"] = send(xt.at[0], xt.at[1], xt_ss.at[0], xt_rs.at[0], other_core)
        flight["chip"] = send(xt.at[0], xt.at[2], xt_ss.at[1], xt_rs.at[1], x_lo_peer)

    def pass_features():
        flight["chip"].wait_recv()
        flight["pass"] = send(xt.at[2], xt.at[3], xt_ss.at[2], xt_rs.at[2], other_core)

    def partial_input_grad(i):
        input_block(i, to_buffer(pc_s if i % 2 == 0 else pp_s, i // 2))
        if i % 2 == 0:
            k = i // 2
            flight["pc", k] = send(pc_s.at[k], pc_r.at[k], pc_ss.at[k], pc_rs.at[k], other_core)

    def chip_sum():
        flight["pc", 0].wait_recv()

        def body(rows):
            pp_s[0, rows, :] = pp_s[0, rows, :] + pc_r[0, rows, :]

        rows_loop(body)
        flight["pp"] = send(pp_s.at[0], pp_r.at[0], pp_ss.at[0], pp_rs.at[0], x_lo_peer)

    def input_grad_sum():
        flight["pc", 1].wait_recv()
        flight["pp"].wait_recv()

        def body(rows):
            total = pp_s[1, rows, :] + pc_r[1, rows, :] + pp_r[0, rows, :]
            ig_buf[rows, :] = total.astype(BF16)

        rows_loop(body)
        write_ig.start()

    load_x.wait()
    xt[0] = (x_in[...] * jnp.array(LIFT, BF16)).T
    load_c.wait()
    first = [at for at in ORDER if at[0] == "mg" and at[1] == at[3] == 0]
    for at in first:
        grad_block(*at[1:])
    for stage, *at in ORDER:
        if stage == "hz0" and at[0] == 0 and at[2] != "f":
            if not plan_of(stage, "r")[at[2]][2]:
                message(stage, *at, only_encode=True)
    pl.semaphore_wait(barrier, len(partners))

    waits = {(0, 1): "core", (1, 1): "pass"}
    waited = set()
    for what, *at in ORDER:
        if what == "sendx":
            send_features()
        elif what == "fwd":
            pass_features()
        elif what[:2] == "ig":
            partial_input_grad(int(what[2]))
        elif what == "iadd":
            chip_sum()
        elif what == "ifin":
            input_grad_sum()
        elif what == "mg":
            ph, s, block = at
            if ph == block == 0:
                continue
            key = waits.get((ph, block))
            if key and key not in waited:
                flight[key].wait_recv()
                waited.add(key)
            grad_block(ph, s, block)
        elif what == "xo":
            own_across(STAGES[STREAMS[at[0]][at[1]][0]][-1], *at)
        elif at[2] == "f":
            (last_finish if what in LAST else finish)(what, *at[:2])
        else:
            message(what, *at)
    write_ig.wait()
    for copy in sends:
        copy.wait_send()
    for ph, s, kind, *_ in streams():

        @pl.when(mine != ph)
        def _():
            own_part(STAGES[kind][-1], ph, s)[2].wait_send()


def reduce_all(norm, inputs, cotangent, weight):
    dma = pltpu.SemaphoreType.DMA
    nm = lambda *s: pltpu.VMEM(s, BF16)
    rings = []
    for _, _, kind, _, width, way in streams():
        for stage in STAGES[kind]:
            plan, count = plan_of(stage, way), COUNT[stage]
            sent = came = len(plan)
            if stage in LAST:
                sent, came = sent + 1, came + len(ends_of(plan)) + 1
            rings += [nm(sent, count, 32, width), nm(came, count, 32, width), dma((sent,)), dma((came,))]
    any_ = pl.BlockSpec(memory_space=pl.ANY)
    vm = pl.BlockSpec(memory_space=pltpu.VMEM)
    return pl.pallas_call(
        lambda *refs: kernel(norm, *refs),
        out_shape=(
            jax.ShapeDtypeStruct((32, COLS), F32),
            jax.ShapeDtypeStruct((TOK, FEAT), BF16),
        ),
        in_specs=[any_, any_, any_],
        out_specs=(vm, any_),
        scratch_shapes=[
            nm(TOK, FEAT), nm(4, FEAT, TOK), nm(TOK, COLS), nm(4, FEAT, COLS),
            pltpu.VMEM((2, 4, 8, 32, COLS), F32),
            pltpu.VMEM((2, TOK, FEAT), F32), pltpu.VMEM((2, TOK, FEAT), F32),
            pltpu.VMEM((2, TOK, FEAT), F32), pltpu.VMEM((1, TOK, FEAT), F32),
            dma((6,)), dma((3,)), dma((3,)),
            dma((2,)), dma((2,)), dma((1,)), dma((1,)),
            *rings,
            nm(TOK, FEAT), dma,
        ],
        compiler_params=pltpu.CompilerParams(
            collective_id=1, has_side_effects=True, vmem_limit_bytes=60 * 2**20
        ),
        cost_estimate=pl.CostEstimate(flops=7516192768, bytes_accessed=12000000, transcendentals=0),
        name="reduce_all",
    )(inputs, cotangent, weight)


def update_kernel(grad, master, first, second, ig, new_master, new_first, new_second, ig_out):
    ig_out[...] = ig[...]
    out = adamw_update(grad[...], master[...], first[...], second[...])
    new_master[...], new_first[...], new_second[...] = out


def update(grad, master, first, second, input_grad):
    rows, tall = pl.BlockSpec((16, COLS), lambda i: (i, 0)), pl.BlockSpec((256, FEAT), lambda i: (i, 0))
    like = lambda a: jax.ShapeDtypeStruct(a.shape, a.dtype)
    return pl.pallas_call(
        update_kernel,
        out_shape=(like(master), like(first), like(second), like(input_grad)),
        grid=(2,),
        in_specs=[rows, rows, rows, rows, tall],
        out_specs=(rows, rows, rows, tall),
        name="update",
    )(grad, master, first, second, input_grad)


def local(inputs, cotangent, weight, master, first_moment, second_moment):
    token_count = inputs.shape[0]
    norm = float(lax.axis_size("dp") * token_count) ** (-0.5) / LIFT
    grad, input_grad = reduce_all(norm, inputs, cotangent, weight)
    out = update(grad, master, first_moment, second_moment, input_grad)
    new_master, new_first, new_second, input_grad = out
    return (input_grad, new_master, new_first, new_second)


def solution(mesh):
    split = P("dp", "fsdp")
    in_specs = (split, split, P(None, "fsdp"), split, split, split)
    return jax.shard_map(
        local, mesh=mesh, in_specs=in_specs, out_specs=(split,) * 4, check_vma=False
    )
```
